32 devices in a mesh: dp: 4 (over z), fsdp: 8 (over y, x, core).
Axes of the slice: x: 2, y: 2, z: 4, core: 2. Of those that a mesh axis runs over, the one named last changes fastest.
Arguments:
- out_grad: bfloat16 [256, 4096], P(('dp', 'fsdp')), may hold values from -6 to 6
- gate_pre: bfloat16 [256, 14848], P('dp', 'fsdp'), may hold values from -6 to 6
- up_pre: bfloat16 [256, 14848], P('dp', 'fsdp'), may hold values from -6 to 6
- down_weight: bfloat16 [14848, 4096], P('fsdp', 'dp'), may hold values from -0.09375 to 0.09375
- momentum: float32 [4, 14848, 256], P('dp', 'fsdp'), may hold values from -6 to 6
- band_index: int32 [4, 14848, 32], P('dp', 'fsdp'), may hold values from 0 to 255, as said below
- band_count: int32 [4, 14848], P('dp', 'fsdp'), may hold values from 1 to 32, as said below
Outputs:
- gate_grad: bfloat16 [256, 14848], P('dp', 'fsdp')
- up_grad: bfloat16 [256, 14848], P('dp', 'fsdp')
- new_momentum: float32 [4, 14848, 256], P('dp', 'fsdp')
- update: float32 [14848, 256], P('fsdp')
The draws below stay inside these ranges and needn't reach their ends.
Inputs may be any that keep to these rules, and one draw needn't show every extreme that they name: `band_index`: for each worker and block the 32 entries of the list are different frequencies. `band_count`: on every worker some block uses all 32 entries and some block uses one.
All inputs are finite; a program needn't handle non-finite values.
Results may differ from the reference program's by a relative error of at most 0.0019.
Values may be sent and summed in bfloat16 or wider, within the bound.
A program may use at most 64 MiB of HBM per device.

```python
import math
import jax
import jax.numpy as jnp
from jax import lax

HIDDEN_SIZE = 14848
FEATURES = 4096
COLUMNS = 256
BLOCK_LEN = 256
BAND_SLOTS = 32
TOK_WORKER = 64
TOKENS = 256
BLOCKS = 14848
N_DP = 4


def draw_band_index(key, part):
    scores = jax.random.randint(key, (N_DP, BLOCKS, BLOCK_LEN), 0, 1 << 20)
    scores = scores * BLOCK_LEN + jnp.arange(BLOCK_LEN, dtype=jnp.int32)[None, None, :]
    ordering = jnp.argsort(scores, axis=2)
    return ordering[:, :, :BAND_SLOTS].astype(jnp.int32)


def draw_band_count(key, part):
    split_keys = jax.random.split(jax.random.fold_in(key, 17), 4)
    ranking = jax.random.permutation(split_keys[0], N_DP).astype(jnp.int32)
    lowest = 1 + ranking * (BAND_SLOTS - 1) // N_DP
    spread = BAND_SLOTS + 1 - lowest
    raw_draw = jax.random.randint(split_keys[1], (N_DP, BLOCKS), 0, 1 << 20)
    counts = raw_draw % spread[:, None] + lowest[:, None]
    full_at = jax.random.randint(split_keys[2], (N_DP,), 0, BLOCKS)
    one_at = (full_at + 1 + jax.random.randint(split_keys[3], (N_DP,), 0, BLOCKS - 1)) % BLOCKS
    positions = jnp.arange(BLOCKS, dtype=jnp.int32)[None, :]
    counts = jnp.where(positions == full_at[:, None], BAND_SLOTS, counts)
    counts = jnp.where(positions == one_at[:, None], 1, counts)
    return counts.astype(jnp.int32)


def block_levels(own_key, shape, pieces, smallest, high):
    def one(dim, blocks):
        steps = jax.random.uniform(jax.random.fold_in(jax.random.fold_in(own_key, 6), dim), (blocks,), jnp.float32, smallest / len(pieces), high / len(pieces))
        return jnp.repeat(jnp.exp(steps), shape[dim] // blocks).reshape((-1,) + (1,) * (len(shape) - dim - 1))

    gain = one(*pieces[0])
    for cut in pieces[1:]:
        gain = gain * one(*cut)
    return gain


def centred(rng, extent, deviation, bound, cuts=(), kind=jnp.bfloat16):
    factor_of = block_levels(rng, extent, cuts, -0.22, 0.18) if cuts else 1.0
    drawn = jax.random.normal(rng, extent, jnp.float32) * deviation * factor_of
    return jnp.minimum(jnp.maximum(drawn, -bound), bound).astype(kind)


def setup_inputs(seed: int = 0) -> dict:
    seeds = jax.random.split(jax.random.key(seed), 8)
    out_grad = centred(seeds[0], (TOKENS, FEATURES), 1.0, 6.0, ((0, 32),))
    gate_pre = centred(seeds[1], (TOKENS, HIDDEN_SIZE), 1.0, 6.0, ((0, 4), (1, 8)))
    up_pre = centred(seeds[2], (TOKENS, HIDDEN_SIZE), 1.0, 6.0, ((0, 4), (1, 8)))
    down_weight = centred(seeds[3], (HIDDEN_SIZE, FEATURES), FEATURES ** -0.5, 0.09375, ((0, 8), (1, 4)))
    momentum = centred(seeds[4], (N_DP, HIDDEN_SIZE, COLUMNS), 1.0, 6.0, ((0, 4), (1, 8)), jnp.float32)
    band_index = draw_band_index(jax.random.fold_in(seeds[7], 71), 0)
    band_count = draw_band_count(jax.random.fold_in(seeds[7], 71), 0)
    return {"out_grad": out_grad, "gate_pre": gate_pre, "up_pre": up_pre, "down_weight": down_weight, "momentum": momentum, "band_index": band_index, "band_count": band_count}


momentum_decay = 0.9

def cosine_matrix(length):
    frequency = jnp.arange(length, dtype=jnp.int32).astype(jnp.float32)[:, None]
    position = jnp.arange(length, dtype=jnp.int32).astype(jnp.float32)[None, :]
    angles = math.pi * (position + 0.5) * frequency / length
    row_weight = jnp.where(frequency == 0.0, math.sqrt(1.0 / length), math.sqrt(2.0 / length))
    return jnp.cos(angles) * row_weight

def reference(out_grad, gate_pre, up_pre, down_weight, momentum, band_index, band_count):
    gate_float = gate_pre.astype(jnp.float32)
    up_float = up_pre.astype(jnp.float32)
    sigmoid_gate = jax.nn.sigmoid(gate_float)
    activation = gate_float * sigmoid_gate
    hidden = (activation * up_float).astype(jnp.bfloat16)
    hidden_grad = jnp.dot(out_grad, down_weight.T, preferred_element_type=jnp.float32)
    up_grad = (hidden_grad * activation).astype(jnp.bfloat16)
    gate_grad = (hidden_grad * up_float * sigmoid_gate * (1.0 + gate_float * (1.0 - sigmoid_gate))).astype(jnp.bfloat16)
    grad_scale = 1.0 / math.sqrt(TOK_WORKER)
    hidden_workers = hidden.reshape(N_DP, TOK_WORKER, HIDDEN_SIZE)
    window_workers = out_grad[:, :COLUMNS].reshape(N_DP, TOK_WORKER, COLUMNS)

    def worker_grad(member_pair):
        return jnp.dot(member_pair[0].T, member_pair[1], preferred_element_type=jnp.float32) * grad_scale
    worker_grads = lax.map(worker_grad, (hidden_workers, window_workers))
    cosine_table = cosine_matrix(BLOCK_LEN)
    mixed = momentum_decay * momentum + worker_grads
    blocked = mixed.reshape(N_DP, BLOCKS, BLOCK_LEN)
    frequency = jnp.arange(BLOCK_LEN, dtype=jnp.int32)
    slot_ids = jnp.arange(BAND_SLOTS, dtype=jnp.int32)

    def one_worker(member):
        rows_blocked, slot_list, counts = member
        spectrum = jnp.dot(rows_blocked, cosine_table.T, precision=lax.Precision.HIGHEST)
        picked = jnp.take_along_axis(spectrum, slot_list, axis=1)
        band_values = jnp.where(slot_ids[None, :] < counts[:, None], picked, 0.0)
        own_spectrum = lax.optimization_barrier(jnp.sum(jnp.where(slot_list[:, :, None] == frequency[None, None, :], band_values[:, :, None], 0.0), axis=1))
        momentum_kept = rows_blocked - jnp.dot(own_spectrum, cosine_table, precision=lax.Precision.HIGHEST)
        return (momentum_kept, own_spectrum)
    kept_all, sent_all = lax.map(one_worker, (blocked, band_index, band_count))
    averaged = lax.optimization_barrier(jnp.sum(sent_all, axis=0)) / N_DP
    update = jnp.dot(averaged, cosine_table, precision=lax.Precision.HIGHEST).reshape(HIDDEN_SIZE, COLUMNS)
    new_momentum = kept_all.reshape(N_DP, HIDDEN_SIZE, COLUMNS)
    return (gate_grad, up_grad, new_momentum, update)
```

```python
import math

import jax
import jax.numpy as jnp
from jax import lax
from jax.sharding import PartitionSpec as P

momentum_decay = 0.9


def cosine_matrix(length):
    frequency = jnp.arange(length, dtype=jnp.int32).astype(jnp.float32)[:, None]
    position = jnp.arange(length, dtype=jnp.int32).astype(jnp.float32)[None, :]
    angles = math.pi * (position + 0.5) * frequency / length
    row_weight = jnp.where(frequency == 0.0, math.sqrt(1.0 / length), math.sqrt(2.0 / length))
    return jnp.cos(angles) * row_weight


def band_mask(slot_list, counts, length):
    slots = slot_list.T
    slot_ids = jnp.arange(slots.shape[0], dtype=jnp.int32)
    bits = jnp.where(slot_ids[:, None] < counts[None, :], jnp.left_shift(1, slots & 7), 0)
    groups = length // 8
    group = jnp.arange(groups, dtype=jnp.int32)
    group_bytes = jnp.sum(
        jnp.where((slots >> 3)[None, :, :] == group[:, None, None], bits[None, :, :], 0), axis=1
    )
    frequency = jnp.arange(length, dtype=jnp.int32)
    spread = ((frequency >> 3)[None, :] == group[:, None]).astype(jnp.bfloat16)
    expanded = lax.dot_general(
        group_bytes.astype(jnp.bfloat16),
        spread,
        (((0,), (0,)), ((), ())),
        preferred_element_type=jnp.float32,
    )
    return ((expanded.astype(jnp.int32) >> (frequency & 7)[None, :]) & 1) == 1


def per_device(out_grad, gate_pre, up_pre, down_weight, momentum, band_index, band_count):
    worker_rows = gate_pre.shape[0]
    own_rows = gate_pre.shape[1]
    window = momentum.shape[2]
    workers = lax.axis_size("dp")
    block_count = band_index.shape[1]
    length = own_rows * window // block_count
    features = down_weight.shape[1]
    token_rows = out_grad.shape[0]

    window_grad = lax.all_gather(out_grad[:, :window], "fsdp", axis=0, tiled=True)
    by_worker = lax.all_to_all(
        out_grad.reshape(token_rows, workers, features).transpose(1, 0, 2),
        "dp",
        split_axis=0,
        concat_axis=0,
        tiled=True,
    )
    all_grad = lax.all_gather(by_worker, "fsdp", axis=1, tiled=True)
    partial_grad = lax.dot_general(
        all_grad.reshape(workers * worker_rows, features),
        down_weight,
        (((1,), (1,)), ((), ())),
        preferred_element_type=jnp.float32,
    )
    hidden_grad = lax.psum_scatter(partial_grad, "dp", scatter_dimension=0, tiled=True)

    gate_float = gate_pre.astype(jnp.float32)
    up_float = up_pre.astype(jnp.float32)
    sigmoid_gate = jax.nn.sigmoid(gate_float)
    activation = gate_float * sigmoid_gate
    hidden = (activation * up_float).astype(jnp.bfloat16)
    up_grad = (hidden_grad * activation).astype(jnp.bfloat16)
    gate_grad = (
        hidden_grad * up_float * sigmoid_gate * (1.0 + gate_float * (1.0 - sigmoid_gate))
    ).astype(jnp.bfloat16)

    grad_scale = 1.0 / math.sqrt(worker_rows)
    worker_grad = (
        lax.dot_general(
            hidden, window_grad, (((0,), (0,)), ((), ())), preferred_element_type=jnp.float32
        )
        * grad_scale
    )
    cosine_table = cosine_matrix(length)
    momentum_mixed = momentum_decay * momentum[0] + worker_grad
    blocked = momentum_mixed.reshape(block_count, length)
    spectrum = jnp.dot(blocked, cosine_table.T, precision=lax.Precision.HIGHEST)
    own_spectrum = jnp.where(band_mask(band_index[0], band_count[0], length), spectrum, 0.0)
    total = lax.psum_scatter(own_spectrum, "dp", scatter_dimension=0, tiled=True)
    momentum_kept = blocked - jnp.dot(
        own_spectrum, cosine_table, precision=lax.Precision.HIGHEST
    )
    part = jnp.dot(total / workers, cosine_table, precision=lax.Precision.HIGHEST)
    update = lax.all_gather(part, "dp", axis=0, tiled=True)
    return (
        gate_grad,
        up_grad,
        momentum_kept.reshape(1, own_rows, window),
        update.reshape(own_rows, window),
    )


def solution(mesh):
    placed = (
        P(("dp", "fsdp"), None),
        P("dp", "fsdp"),
        P("dp", "fsdp"),
        P("fsdp", "dp"),
        P("dp", "fsdp", None),
        P("dp", "fsdp", None),
        P("dp", "fsdp"),
    )
    return jax.shard_map(
        per_device,
        mesh=mesh,
        in_specs=placed,
        out_specs=(P("dp", "fsdp"), P("dp", "fsdp"), P("dp", "fsdp", None), P("fsdp", None)),
        check_vma=False,
    )
```

```python
import math

import jax
import jax.numpy as jnp
from jax import lax
from jax.experimental import pallas as pl
from jax.experimental.pallas import tpu as pltpu
from jax.sharding import PartitionSpec as P

momentum_decay = 0.9


def cosine_matrix(length):
    frequency = jnp.arange(length, dtype=jnp.int32).astype(jnp.float32)[:, None]
    position = jnp.arange(length, dtype=jnp.int32).astype(jnp.float32)[None, :]
    angles = math.pi * (position + 0.5) * frequency / length
    row_weight = jnp.where(frequency == 0.0, math.sqrt(1.0 / length), math.sqrt(2.0 / length))
    return jnp.cos(angles) * row_weight


lanes = 128


def sorted_slots(slot_list, counts, length):
    slots = slot_list.T
    slot_ids = jnp.arange(slots.shape[0], dtype=jnp.int32)
    keys = jnp.where(slot_ids[:, None] < counts[None, :], slots, length + slot_ids[:, None])
    rank = jnp.sum((keys[:, None, :] < keys[None, :, :]).astype(jnp.int32), axis=0)
    ordered = jnp.sum(
        jnp.where(rank[:, None, :] == slot_ids[None, :, None], keys[:, None, :], 0), axis=0
    )
    return jnp.minimum(ordered, length)


def group_bytes(slots, length):
    group = jnp.arange(length // 8, dtype=jnp.int32)
    bits = jnp.left_shift(1, slots & 7)
    return jnp.sum(
        jnp.where(
            (slots >> 3)[..., None, :, :] == group[:, None, None], bits[..., None, :, :], 0
        ),
        axis=-2,
    ).astype(jnp.bfloat16)


def spread_matrix(length):
    group = jnp.arange(length // 8, dtype=jnp.int32)
    frequency = jnp.arange(length, dtype=jnp.int32)
    return ((frequency >> 3)[None, :] == group[:, None]).astype(jnp.bfloat16)


def below_matrix(length):
    frequency = jnp.arange(length, dtype=jnp.int32)
    return (frequency[:, None] < frequency[None, :]).astype(jnp.bfloat16)


def lane_pick(values, places):
    return jnp.take_along_axis(values, places, axis=1, mode="promise_in_bounds")


def tile_rows(rows):
    return rows // 4 if rows % 64 == 0 else rows


def pick_kernel(spectrum_ref, places_ref, picked_ref):
    places = places_ref[...]
    inside = places & (lanes - 1)
    picked = jnp.zeros(places.shape, jnp.float32)
    for start in range(0, spectrum_ref.shape[1], lanes):
        here = lane_pick(spectrum_ref[:, start : start + lanes], inside)
        picked = jnp.where((places >= start) & (places < start + lanes), here, picked)
    picked_ref[...] = picked


def pick(spectrum, places):
    rows, length = spectrum.shape
    tile = tile_rows(rows)
    return pl.pallas_call(
        pick_kernel,
        grid=(rows // tile,),
        out_shape=jax.ShapeDtypeStruct((rows, lanes), jnp.float32),
        in_specs=[
            pl.BlockSpec((tile, length), lambda i: (i, 0)),
            pl.BlockSpec((tile, lanes), lambda i: (i, 0)),
        ],
        out_specs=pl.BlockSpec((tile, lanes), lambda i: (i, 0)),
        compiler_params=pltpu.CompilerParams(vmem_limit_bytes=24 * 2**20),
        cost_estimate=pl.CostEstimate(
            flops=rows * length * 4, bytes_accessed=rows * length * 8, transcendentals=0
        ),
    )(spectrum, places)


def update_kernel(values_ref, bytes_ref, spread_ref, below_ref, table_ref, update_ref):
    workers, tile = values_ref.shape[0], values_ref.shape[1]
    length = table_ref.shape[0]
    shift = lax.broadcasted_iota(jnp.int32, (tile, length), 1) & 7
    total = [jnp.zeros((tile, lanes), jnp.float32) for _ in range(length // lanes)]
    for worker in range(workers):
        expanded = jnp.dot(
            bytes_ref[worker], spread_ref[...], preferred_element_type=jnp.float32
        ).astype(jnp.int32)
        used = (expanded >> shift) & 1
        rank = jnp.dot(
            used.astype(jnp.float32).astype(jnp.bfloat16),
            below_ref[...],
            preferred_element_type=jnp.float32,
        ).astype(jnp.int32)
        values = values_ref[worker]
        values = jnp.concatenate(
            [values, jnp.zeros((tile, lanes - values.shape[1]), jnp.float32)], axis=1
        )
        for part in range(length // lanes):
            columns = slice(part * lanes, (part + 1) * lanes)
            here = lane_pick(values, rank[:, columns] & (lanes - 1))
            total[part] = total[part] + jnp.where(used[:, columns] == 1, here, 0.0)
    averaged = jnp.concatenate(total, axis=1) * (1.0 / workers)
    update_ref[...] = jnp.dot(
        averaged,
        table_ref[...],
        precision=lax.Precision.HIGHEST,
        preferred_element_type=jnp.float32,
    )


def summed_update(values, group_rows, table):
    workers, rows, slot_count = values.shape
    length = table.shape[0]
    groups = group_rows.shape[2]
    tile = tile_rows(rows)
    whole = lambda i: (0, 0)
    return pl.pallas_call(
        update_kernel,
        grid=(rows // tile,),
        out_shape=jax.ShapeDtypeStruct((rows, length), jnp.float32),
        in_specs=[
            pl.BlockSpec((workers, tile, slot_count), lambda i: (0, i, 0)),
            pl.BlockSpec((workers, tile, groups), lambda i: (0, i, 0)),
            pl.BlockSpec((groups, length), whole),
            pl.BlockSpec((length, length), whole),
            pl.BlockSpec((length, length), whole),
        ],
        out_specs=pl.BlockSpec((tile, length), lambda i: (i, 0)),
        compiler_params=pltpu.CompilerParams(vmem_limit_bytes=40 * 2**20),
        cost_estimate=pl.CostEstimate(
            flops=rows * length * length * 16, bytes_accessed=rows * length * 16, transcendentals=0
        ),
    )(values, group_rows, spread_matrix(length), below_matrix(length), table)


def per_device(out_grad, gate_pre, up_pre, down_weight, momentum, band_index, band_count):
    worker_rows = gate_pre.shape[0]
    own_rows = gate_pre.shape[1]
    window = momentum.shape[2]
    workers = lax.axis_size("dp")
    block_count = band_index.shape[1]
    length = own_rows * window // block_count
    features = down_weight.shape[1]
    token_rows = out_grad.shape[0]

    slots = sorted_slots(band_index[0], band_count[0], length)
    slot_count = slots.shape[0]
    all_slots = lax.all_gather(slots.astype(jnp.bfloat16), "dp", axis=0)
    all_bytes = group_bytes(all_slots.astype(jnp.int32), length).transpose(0, 2, 1)
    places = jnp.pad(slots.T, ((0, 0), (0, lanes - slot_count)), constant_values=length)
    frequency = jnp.arange(length, dtype=jnp.int32)
    expanded = lax.dot_general(
        group_bytes(slots, length),
        spread_matrix(length),
        (((0,), (0,)), ((), ())),
        preferred_element_type=jnp.float32,
    )
    mask = ((expanded.astype(jnp.int32) >> (frequency & 7)[None, :]) & 1) == 1

    window_grad = lax.all_gather(out_grad[:, :window], "fsdp", axis=0, tiled=True)
    by_worker = lax.all_to_all(
        out_grad.reshape(token_rows, workers, features).transpose(1, 0, 2),
        "dp",
        split_axis=0,
        concat_axis=0,
        tiled=True,
    )
    all_grad = lax.all_gather(by_worker, "fsdp", axis=1, tiled=True)
    partial_grad = lax.dot_general(
        all_grad.reshape(workers * worker_rows, features),
        down_weight,
        (((1,), (1,)), ((), ())),
        preferred_element_type=jnp.float32,
    )
    hidden_grad = lax.psum_scatter(partial_grad, "dp", scatter_dimension=0, tiled=True)

    gate_float = gate_pre.astype(jnp.float32)
    up_float = up_pre.astype(jnp.float32)
    sigmoid_gate = jax.nn.sigmoid(gate_float)
    activation = gate_float * sigmoid_gate
    hidden = (activation * up_float).astype(jnp.bfloat16)
    up_grad = (hidden_grad * activation).astype(jnp.bfloat16)
    gate_grad = (
        hidden_grad * up_float * sigmoid_gate * (1.0 + gate_float * (1.0 - sigmoid_gate))
    ).astype(jnp.bfloat16)

    grad_scale = 1.0 / math.sqrt(worker_rows)
    worker_grad = (
        lax.dot_general(
            hidden, window_grad, (((0,), (0,)), ((), ())), preferred_element_type=jnp.float32
        )
        * grad_scale
    )
    cosine_table = cosine_matrix(length)
    momentum_mixed = momentum_decay * momentum[0] + worker_grad
    blocked = momentum_mixed.reshape(block_count, length)
    spectrum = jnp.dot(blocked, cosine_table.T, precision=lax.Precision.HIGHEST)
    picked = pick(spectrum, places)[:, :slot_count].T
    all_values = lax.all_gather(picked, "dp", axis=0)
    own_spectrum = jnp.where(mask, spectrum, 0.0)
    momentum_kept = blocked - jnp.dot(
        own_spectrum, cosine_table, precision=lax.Precision.HIGHEST
    )
    update = summed_update(all_values.transpose(0, 2, 1), all_bytes, cosine_table)
    return (
        gate_grad,
        up_grad,
        momentum_kept.reshape(1, own_rows, window),
        update.reshape(own_rows, window),
    )


def solution(mesh):
    placed = (
        P(("dp", "fsdp"), None),
        P("dp", "fsdp"),
        P("dp", "fsdp"),
        P("fsdp", "dp"),
        P("dp", "fsdp", None),
        P("dp", "fsdp", None),
        P("dp", "fsdp"),
    )
    return jax.shard_map(
        per_device,
        mesh=mesh,
        in_specs=placed,
        out_specs=(P("dp", "fsdp"), P("dp", "fsdp"), P("dp", "fsdp", None), P("fsdp", None)),
        check_vma=False,
    )
```

```python
import math

import jax
import jax.numpy as jnp
from jax import lax
from jax.experimental import pallas as pl
from jax.experimental.pallas import tpu as pltpu
from jax.sharding import PartitionSpec as P

momentum_decay = 0.9


def cosine_matrix(length):
    frequency = jnp.arange(length, dtype=jnp.int32).astype(jnp.float32)[:, None]
    position = jnp.arange(length, dtype=jnp.int32).astype(jnp.float32)[None, :]
    angles = math.pi * (position + 0.5) * frequency / length
    row_weight = jnp.where(frequency == 0.0, math.sqrt(1.0 / length), math.sqrt(2.0 / length))
    return jnp.cos(angles) * row_weight


lanes = 128


def sorted_slots(slot_list, counts, length):
    slots = slot_list.T
    slot_ids = jnp.arange(slots.shape[0], dtype=jnp.int32)
    keys = jnp.where(slot_ids[:, None] < counts[None, :], slots, length + slot_ids[:, None])
    rank = jnp.sum((keys[:, None, :] < keys[None, :, :]).astype(jnp.int32), axis=0)
    ordered = jnp.sum(
        jnp.where(rank[:, None, :] == slot_ids[None, :, None], keys[:, None, :], 0), axis=0
    )
    return jnp.minimum(ordered, length)


def group_bytes(slots, length):
    group = jnp.arange(length // 8, dtype=jnp.int32)
    bits = jnp.left_shift(1, slots & 7)
    return jnp.sum(
        jnp.where(
            (slots >> 3)[..., None, :, :] == group[:, None, None], bits[..., None, :, :], 0
        ),
        axis=-2,
    ).astype(jnp.bfloat16)


def spread_matrix(length):
    group = jnp.arange(length // 8, dtype=jnp.int32)
    frequency = jnp.arange(length, dtype=jnp.int32)
    return ((frequency >> 3)[None, :] == group[:, None]).astype(jnp.bfloat16)


def below_matrix(length):
    frequency = jnp.arange(length, dtype=jnp.int32)
    return (frequency[:, None] < frequency[None, :]).astype(jnp.bfloat16)


def lane_pick(values, places):
    return jnp.take_along_axis(values, places, axis=1, mode="promise_in_bounds")


def from_each(block, workers):
    return [block] + [
        lax.ppermute(block, "dp", [(i, (i + step) % workers) for i in range(workers)])
        for step in range(1, workers)
    ]


def tile_rows(rows):
    return rows // 4 if rows % 64 == 0 else rows


def pick_kernel(spectrum_ref, places_ref, picked_ref):
    places = places_ref[...]
    inside = places & (lanes - 1)
    picked = jnp.zeros(places.shape, jnp.float32)
    for start in range(0, spectrum_ref.shape[1], lanes):
        here = lane_pick(spectrum_ref[:, start : start + lanes], inside)
        picked = jnp.where((places >= start) & (places < start + lanes), here, picked)
    picked_ref[...] = picked


def pick(spectrum, places):
    rows, length = spectrum.shape
    tile = tile_rows(rows)
    return pl.pallas_call(
        pick_kernel,
        grid=(rows // tile,),
        out_shape=jax.ShapeDtypeStruct((rows, lanes), jnp.float32),
        in_specs=[
            pl.BlockSpec((tile, length), lambda i: (i, 0)),
            pl.BlockSpec((tile, lanes), lambda i: (i, 0)),
        ],
        out_specs=pl.BlockSpec((tile, lanes), lambda i: (i, 0)),
        compiler_params=pltpu.CompilerParams(vmem_limit_bytes=24 * 2**20),
        cost_estimate=pl.CostEstimate(
            flops=rows * length * 4, bytes_accessed=rows * length * 8, transcendentals=0
        ),
    )(spectrum, places)


def update_kernel(own_ref, values_ref, bytes_ref, spread_ref, below_ref, table_ref, update_ref):
    workers, tile = values_ref.shape[0], values_ref.shape[1]
    length = table_ref.shape[0]
    shift = lax.broadcasted_iota(jnp.int32, (tile, length), 1) & 7
    total = [jnp.zeros((tile, lanes), jnp.float32) for _ in range(length // lanes)]
    for worker in range(workers):
        held = lax.rem(own_ref[0] - worker + workers, workers)
        expanded = jnp.dot(
            bytes_ref[held], spread_ref[...], preferred_element_type=jnp.float32
        ).astype(jnp.int32)
        used = (expanded >> shift) & 1
        rank = jnp.dot(
            used.astype(jnp.float32).astype(jnp.bfloat16),
            below_ref[...],
            preferred_element_type=jnp.float32,
        ).astype(jnp.int32)
        values = values_ref[held]
        values = jnp.concatenate(
            [values, jnp.zeros((tile, lanes - values.shape[1]), jnp.float32)], axis=1
        )
        for part in range(length // lanes):
            columns = slice(part * lanes, (part + 1) * lanes)
            here = lane_pick(values, rank[:, columns] & (lanes - 1))
            total[part] = total[part] + jnp.where(used[:, columns] == 1, here, 0.0)
    averaged = jnp.concatenate(total, axis=1) * (1.0 / workers)
    update_ref[...] = jnp.dot(
        averaged,
        table_ref[...],
        precision=lax.Precision.HIGHEST,
        preferred_element_type=jnp.float32,
    )


def summed_update(own, values, group_rows, table):
    workers, rows, slot_count = values.shape
    length = table.shape[0]
    groups = group_rows.shape[2]
    tile = tile_rows(rows)
    whole = lambda i: (0, 0)
    return pl.pallas_call(
        update_kernel,
        grid=(rows // tile,),
        out_shape=jax.ShapeDtypeStruct((rows, length), jnp.float32),
        in_specs=[
            pl.BlockSpec(memory_space=pltpu.SMEM),
            pl.BlockSpec((workers, tile, slot_count), lambda i: (0, i, 0)),
            pl.BlockSpec((workers, tile, groups), lambda i: (0, i, 0)),
            pl.BlockSpec((groups, length), whole),
            pl.BlockSpec((length, length), whole),
            pl.BlockSpec((length, length), whole),
        ],
        out_specs=pl.BlockSpec((tile, length), lambda i: (i, 0)),
        compiler_params=pltpu.CompilerParams(vmem_limit_bytes=40 * 2**20),
        cost_estimate=pl.CostEstimate(
            flops=rows * length * length * 16, bytes_accessed=rows * length * 16, transcendentals=0
        ),
    )(own, values, group_rows, spread_matrix(length), below_matrix(length), table)


def per_device(out_grad, gate_pre, up_pre, down_weight, momentum, band_index, band_count):
    worker_rows = gate_pre.shape[0]
    own_rows = gate_pre.shape[1]
    window = momentum.shape[2]
    workers = lax.axis_size("dp")
    block_count = band_index.shape[1]
    length = own_rows * window // block_count
    features = down_weight.shape[1]
    token_rows = out_grad.shape[0]

    by_worker = lax.all_to_all(
        out_grad.reshape(token_rows, workers, features).transpose(1, 0, 2),
        "dp",
        split_axis=0,
        concat_axis=0,
        tiled=True,
    )
    extra = -(-window // features)
    tail = jnp.pad(out_grad[:, :window], ((0, 0), (0, extra * features - window)))
    tail = tail.reshape(token_rows, extra, features).transpose(1, 0, 2)
    gathered = lax.all_gather(
        jnp.concatenate([by_worker, tail], axis=0), "fsdp", axis=1, tiled=True
    )
    partial_grad = lax.dot_general(
        gathered[:workers].reshape(workers * worker_rows, features),
        down_weight,
        (((1,), (1,)), ((), ())),
        preferred_element_type=jnp.float32,
    )
    _, gathered, momentum, band_index, band_count = lax.optimization_barrier(
        (partial_grad[:1, :1], gathered, momentum, band_index, band_count)
    )
    hidden_grad = lax.psum_scatter(partial_grad, "dp", scatter_dimension=0, tiled=True)
    window_grad = jnp.concatenate([gathered[workers + i] for i in range(extra)], axis=1)
    window_grad = window_grad[:, :window]

    slots = sorted_slots(band_index[0], band_count[0], length)
    slot_count = slots.shape[0]
    all_slots = from_each(slots.astype(jnp.bfloat16), workers)
    own_bytes = group_bytes(slots, length)
    all_bytes = jnp.stack(
        [own_bytes] + [group_bytes(got.astype(jnp.int32), length) for got in all_slots[1:]]
    ).transpose(0, 2, 1)
    places = jnp.pad(slots.T, ((0, 0), (0, lanes - slot_count)), constant_values=length)
    frequency = jnp.arange(length, dtype=jnp.int32)
    expanded = lax.dot_general(
        own_bytes,
        spread_matrix(length),
        (((0,), (0,)), ((), ())),
        preferred_element_type=jnp.float32,
    )
    mask = ((expanded.astype(jnp.int32) >> (frequency & 7)[None, :]) & 1) == 1

    gate_float = gate_pre.astype(jnp.float32)
    up_float = up_pre.astype(jnp.float32)
    sigmoid_gate = jax.nn.sigmoid(gate_float)
    activation = gate_float * sigmoid_gate
    hidden = (activation * up_float).astype(jnp.bfloat16)
    up_grad = (hidden_grad * activation).astype(jnp.bfloat16)
    gate_grad = (
        hidden_grad * up_float * sigmoid_gate * (1.0 + gate_float * (1.0 - sigmoid_gate))
    ).astype(jnp.bfloat16)

    grad_scale = 1.0 / math.sqrt(worker_rows)
    worker_grad = (
        lax.dot_general(
            hidden, window_grad, (((0,), (0,)), ((), ())), preferred_element_type=jnp.float32
        )
        * grad_scale
    )
    cosine_table = cosine_matrix(length)
    momentum_mixed = momentum_decay * momentum[0] + worker_grad
    blocked = momentum_mixed.reshape(block_count, length)
    spectrum = jnp.dot(blocked, cosine_table.T, precision=lax.Precision.HIGHEST)
    picked = pick(spectrum, places)[:, :slot_count].T
    all_values = jnp.stack(from_each(picked, workers))
    own_spectrum = jnp.where(mask, spectrum, 0.0)
    momentum_kept = blocked - jnp.dot(
        own_spectrum, cosine_table, precision=lax.Precision.HIGHEST
    )
    own = lax.axis_index("dp").astype(jnp.int32).reshape(1)
    update = summed_update(own, all_values.transpose(0, 2, 1), all_bytes, cosine_table)
    return (
        gate_grad,
        up_grad,
        momentum_kept.reshape(1, own_rows, window),
        update.reshape(own_rows, window),
    )


def solution(mesh):
    placed = (
        P(("dp", "fsdp"), None),
        P("dp", "fsdp"),
        P("dp", "fsdp"),
        P("fsdp", "dp"),
        P("dp", "fsdp", None),
        P("dp", "fsdp", None),
        P("dp", "fsdp"),
    )
    return jax.shard_map(
        per_device,
        mesh=mesh,
        in_specs=placed,
        out_specs=(P("dp", "fsdp"), P("dp", "fsdp"), P("dp", "fsdp", None), P("fsdp", None)),
        check_vma=False,
    )
```

```python
import math

import jax
import jax.numpy as jnp
from jax import lax
from jax.experimental import pallas as pl
from jax.experimental.pallas import tpu as pltpu
from jax.sharding import PartitionSpec as P

momentum_decay = 0.9


def cosine_matrix(length):
    frequency = jnp.arange(length, dtype=jnp.int32).astype(jnp.float32)[:, None]
    position = jnp.arange(length, dtype=jnp.int32).astype(jnp.float32)[None, :]
    angles = math.pi * (position + 0.5) * frequency / length
    row_weight = jnp.where(frequency == 0.0, math.sqrt(1.0 / length), math.sqrt(2.0 / length))
    return jnp.cos(angles) * row_weight


lanes = 128


def sorted_slots(slot_list, counts, length):
    slots = slot_list.T
    slot_ids = jnp.arange(slots.shape[0], dtype=jnp.int32)
    keys = jnp.where(slot_ids[:, None] < counts[None, :], slots, length + slot_ids[:, None])
    rank = jnp.sum((keys[:, None, :] < keys[None, :, :]).astype(jnp.int32), axis=0)
    ordered = jnp.sum(
        jnp.where(rank[:, None, :] == slot_ids[None, :, None], keys[:, None, :], 0), axis=0
    )
    return jnp.minimum(ordered, length)


def group_bytes(slots, length):
    group = jnp.arange(length // 8, dtype=jnp.int32)
    bits = jnp.left_shift(1, slots & 7)
    return jnp.sum(
        jnp.where(
            (slots >> 3)[..., None, :, :] == group[:, None, None], bits[..., None, :, :], 0
        ),
        axis=-2,
    ).astype(jnp.bfloat16)


def spread_matrix(length):
    group = jnp.arange(length // 8, dtype=jnp.int32)
    frequency = jnp.arange(length, dtype=jnp.int32)
    return ((frequency >> 3)[None, :] == group[:, None]).astype(jnp.bfloat16)


def below_matrix(length):
    frequency = jnp.arange(length, dtype=jnp.int32)
    return (frequency[:, None] < frequency[None, :]).astype(jnp.bfloat16)


def lane_pick(values, places):
    return jnp.take_along_axis(values, places, axis=1, mode="promise_in_bounds")


def tile_rows(rows):
    return rows // 4 if rows % 64 == 0 else rows


def pick_kernel(spectrum_ref, places_ref, picked_ref):
    places = places_ref[...]
    inside = places & (lanes - 1)
    picked = jnp.zeros(places.shape, jnp.float32)
    for start in range(0, spectrum_ref.shape[1], lanes):
        here = lane_pick(spectrum_ref[:, start : start + lanes], inside)
        picked = jnp.where((places >= start) & (places < start + lanes), here, picked)
    picked_ref[...] = picked


def pick(spectrum, places):
    rows, length = spectrum.shape
    tile = tile_rows(rows)
    return pl.pallas_call(
        pick_kernel,
        grid=(rows // tile,),
        out_shape=jax.ShapeDtypeStruct((rows, lanes), jnp.float32),
        in_specs=[
            pl.BlockSpec((tile, length), lambda i: (i, 0)),
            pl.BlockSpec((tile, lanes), lambda i: (i, 0)),
        ],
        out_specs=pl.BlockSpec((tile, lanes), lambda i: (i, 0)),
        compiler_params=pltpu.CompilerParams(vmem_limit_bytes=24 * 2**20),
        cost_estimate=pl.CostEstimate(
            flops=rows * length * 4, bytes_accessed=rows * length * 8, transcendentals=0
        ),
    )(spectrum, places)


def update_kernel(values_ref, bytes_ref, spread_ref, below_ref, table_ref, update_ref):
    workers, tile = values_ref.shape[0], values_ref.shape[1]
    length = table_ref.shape[0]
    shift = lax.broadcasted_iota(jnp.int32, (tile, length), 1) & 7
    total = [jnp.zeros((tile, lanes), jnp.float32) for _ in range(length // lanes)]
    for worker in range(workers):
        expanded = jnp.dot(
            bytes_ref[worker], spread_ref[...], preferred_element_type=jnp.float32
        ).astype(jnp.int32)
        used = (expanded >> shift) & 1
        rank = jnp.dot(
            used.astype(jnp.float32).astype(jnp.bfloat16),
            below_ref[...],
            preferred_element_type=jnp.float32,
        ).astype(jnp.int32)
        values = values_ref[worker]
        values = jnp.concatenate(
            [values, jnp.zeros((tile, lanes - values.shape[1]), jnp.float32)], axis=1
        )
        for part in range(length // lanes):
            columns = slice(part * lanes, (part + 1) * lanes)
            here = lane_pick(values, rank[:, columns] & (lanes - 1))
            total[part] = total[part] + jnp.where(used[:, columns] == 1, here, 0.0)
    averaged = jnp.concatenate(total, axis=1) * (1.0 / workers)
    update_ref[...] = jnp.dot(
        averaged,
        table_ref[...],
        precision=lax.Precision.HIGHEST,
        preferred_element_type=jnp.float32,
    )


def summed_update(values, group_rows, table):
    workers, rows, slot_count = values.shape
    length = table.shape[0]
    groups = group_rows.shape[2]
    tile = tile_rows(rows)
    whole = lambda i: (0, 0)
    return pl.pallas_call(
        update_kernel,
        grid=(rows // tile,),
        out_shape=jax.ShapeDtypeStruct((rows, length), jnp.float32),
        in_specs=[
            pl.BlockSpec((workers, tile, slot_count), lambda i: (0, i, 0)),
            pl.BlockSpec((workers, tile, groups), lambda i: (0, i, 0)),
            pl.BlockSpec((groups, length), whole),
            pl.BlockSpec((length, length), whole),
            pl.BlockSpec((length, length), whole),
        ],
        out_specs=pl.BlockSpec((tile, length), lambda i: (i, 0)),
        compiler_params=pltpu.CompilerParams(vmem_limit_bytes=40 * 2**20),
        cost_estimate=pl.CostEstimate(
            flops=rows * length * length * 16, bytes_accessed=rows * length * 16, transcendentals=0
        ),
    )(values, group_rows, spread_matrix(length), below_matrix(length), table)


def per_device(out_grad, gate_pre, up_pre, down_weight, momentum, band_index, band_count):
    worker_rows = gate_pre.shape[0]
    own_rows = gate_pre.shape[1]
    window = momentum.shape[2]
    workers = lax.axis_size("dp")
    block_count = band_index.shape[1]
    length = own_rows * window // block_count
    features = down_weight.shape[1]
    token_rows = out_grad.shape[0]

    slots = sorted_slots(band_index[0], band_count[0], length)
    slot_count = slots.shape[0]
    all_slots = lax.all_gather(slots.astype(jnp.bfloat16), "dp", axis=0)
    all_bytes = group_bytes(all_slots.astype(jnp.int32), length).transpose(0, 2, 1)
    places = jnp.pad(slots.T, ((0, 0), (0, lanes - slot_count)), constant_values=length)
    frequency = jnp.arange(length, dtype=jnp.int32)
    expanded = lax.dot_general(
        group_bytes(slots, length),
        spread_matrix(length),
        (((0,), (0,)), ((), ())),
        preferred_element_type=jnp.float32,
    )
    mask = ((expanded.astype(jnp.int32) >> (frequency & 7)[None, :]) & 1) == 1

    by_worker = lax.all_to_all(
        out_grad.reshape(token_rows, workers, features).transpose(1, 0, 2),
        "dp",
        split_axis=0,
        concat_axis=0,
        tiled=True,
    )
    extra = -(-window // features)
    tail = jnp.pad(out_grad[:, :window], ((0, 0), (0, extra * features - window)))
    tail = tail.reshape(token_rows, extra, features).transpose(1, 0, 2)
    gathered = lax.all_gather(
        jnp.concatenate([by_worker, tail], axis=0), "fsdp", axis=1, tiled=True
    )
    partial_grad = lax.dot_general(
        gathered[:workers].reshape(workers * worker_rows, features),
        down_weight,
        (((1,), (1,)), ((), ())),
        preferred_element_type=jnp.float32,
    )
    window_grad = jnp.concatenate([gathered[workers + i] for i in range(extra)], axis=1)
    first = partial_grad[0, 0]
    window_grad = jnp.where(first == first, window_grad[:, :window], 0)
    hidden_grad = lax.psum_scatter(partial_grad, "dp", scatter_dimension=0, tiled=True)

    gate_float = gate_pre.astype(jnp.float32)
    up_float = up_pre.astype(jnp.float32)
    sigmoid_gate = jax.nn.sigmoid(gate_float)
    activation = gate_float * sigmoid_gate
    hidden = (activation * up_float).astype(jnp.bfloat16)
    up_grad = (hidden_grad * activation).astype(jnp.bfloat16)
    gate_grad = (
        hidden_grad * up_float * sigmoid_gate * (1.0 + gate_float * (1.0 - sigmoid_gate))
    ).astype(jnp.bfloat16)

    grad_scale = 1.0 / math.sqrt(worker_rows)
    worker_grad = (
        lax.dot_general(
            hidden, window_grad, (((0,), (0,)), ((), ())), preferred_element_type=jnp.float32
        )
        * grad_scale
    )
    cosine_table = cosine_matrix(length)
    momentum_mixed = momentum_decay * momentum[0] + worker_grad
    blocked = momentum_mixed.reshape(block_count, length)
    spectrum = jnp.dot(blocked, cosine_table.T, precision=lax.Precision.HIGHEST)
    picked = pick(spectrum, places)[:, :slot_count].T
    all_values = lax.all_gather(picked, "dp", axis=0)
    own_spectrum = jnp.where(mask, spectrum, 0.0)
    momentum_kept = blocked - jnp.dot(
        own_spectrum, cosine_table, precision=lax.Precision.HIGHEST
    )
    update = summed_update(all_values.transpose(0, 2, 1), all_bytes, cosine_table)
    return (
        gate_grad,
        up_grad,
        momentum_kept.reshape(1, own_rows, window),
        update.reshape(own_rows, window),
    )


def solution(mesh):
    placed = (
        P(("dp", "fsdp"), None),
        P("dp", "fsdp"),
        P("dp", "fsdp"),
        P("fsdp", "dp"),
        P("dp", "fsdp", None),
        P("dp", "fsdp", None),
        P("dp", "fsdp"),
    )
    return jax.shard_map(
        per_device,
        mesh=mesh,
        in_specs=placed,
        out_specs=(P("dp", "fsdp"), P("dp", "fsdp"), P("dp", "fsdp", None), P("fsdp", None)),
        check_vma=False,
    )
```
